512 devices in a mesh: batch: 16 (over z_hi, y, core), tensor: 32 (over x, z_lo).
Axes of the slice: x: 4, y: 4, z: 16 (z_hi: 2, z_lo: 8; z = z_hi * 8 + z_lo), core: 2. Of those that a mesh axis runs over, the one named last changes fastest.
Arguments:
- tokens: bfloat16 [4096, 4096], P('batch', 'tensor'), may hold values from -6 to 6
- gate_pre: bfloat16 [4096, 14336], P('batch', 'tensor'), may hold values from -8 to 8
- up_pre: bfloat16 [4096, 14336], P('batch', 'tensor'), may hold values from -6 to 6
- down_weight: bfloat16 [14336, 4096], P('tensor'), may hold values from -0.046875 to 0.046875
- tangent_gate: bfloat16 [4096, 14336], P('batch', 'tensor'), may hold values from -0.09375 to 0.09375
- loss_weight: float32 [4096], P('batch'), may hold values from 0.05 to 0.5
Outputs:
- gnvp: float32 [4096, 14336], P('batch', 'tensor')
The draws below stay inside these ranges and needn't reach their ends.
All inputs are finite; a program needn't handle non-finite values.
Results may differ from the reference program's by a relative error of at most 0.025.
Values may be sent and summed in bfloat16 or wider, within the bound.
A program may use at most 64 MiB of HBM per device.

```python
import math
import jax
import jax.numpy as jnp
from jax import lax

D = 4096
FF = 14336
TOK_DEV = 256
TOKENS = 4096
N_BATCH = 16


def strengthened(entries, rng, source, target, blocks, factor):
    owner, partner = [(jnp.arange(entries.shape[position]) // (entries.shape[position] // blocks)).reshape([-1 if axis == position else 1 for axis in range(entries.ndim)]) for position in (source, target)]
    chosen = jax.random.permutation(rng, blocks)[partner]
    strong = (owner == chosen) | (owner == (partner + blocks // 2) % blocks)
    return jnp.where(strong, factor * entries, entries)


def shard_levels(stream_key, shape, shards, low, top_value):
    def one(dim, blocks):
        steps = jax.random.uniform(jax.random.fold_in(jax.random.fold_in(stream_key, 6), dim), (blocks,), jnp.float32, low / len(shards), top_value / len(shards))
        return jnp.repeat(jnp.exp(steps), shape[dim] // blocks).reshape((-1,) + (1,) * (len(shape) - dim - 1))

    loudness = one(*shards[0])
    for cut in shards[1:]:
        loudness = loudness * one(*cut)
    return loudness


def noise(rng, extent, deviation, reach, split=(), dtype=jnp.bfloat16):
    array = deviation * jax.random.normal(rng, extent, jnp.float32)
    if split:
        array = array * shard_levels(rng, extent, split, -0.22, 0.18)
    return jnp.clip(array, -reach, reach).astype(dtype)


def gaussian_with(own_key, dims, scale, limit, cuts, heavy, held_as=jnp.bfloat16):
    array = scale * jax.random.normal(own_key, dims, jnp.float32)
    if cuts:
        array = array * shard_levels(own_key, dims, cuts, -0.22, 0.18)
    return jnp.clip(strengthened(array, jax.random.fold_in(own_key, 3), *heavy), -limit, limit).astype(held_as)


def setup_inputs(seed: int = 0) -> dict:
    arg_keys = jax.random.split(jax.random.key(seed), 7)
    tokens = gaussian_with(arg_keys[0], (TOKENS, D), 1.0, 6.0, ((0, 16), (1, 32)), (0, 1, 32, 2.75))
    gate_pre = noise(arg_keys[1], (TOKENS, FF), 1.5, 8.0, ((0, 16), (1, 32)))
    up_pre = noise(arg_keys[2], (TOKENS, FF), 1.0, 6.0, ((0, 16), (1, 32)))
    down_weight = noise(arg_keys[3], (FF, D), FF ** -0.5, 0.046875, ((0, 32),))
    tangent_gate = noise(arg_keys[4], (D, FF), D ** -0.5, 0.09375, ((0, 16), (1, 32)))
    loss_weight = jnp.clip(jnp.exp(math.log(0.5) - 2.3025851 * jax.random.uniform(arg_keys[5], (TOKENS,), jnp.float32) ** shard_levels(arg_keys[5], (TOKENS,), ((0, 16),), -0.2, 0.2)), 0.05, 0.5)
    return dict(tokens=tokens, gate_pre=gate_pre, up_pre=up_pre, down_weight=down_weight, tangent_gate=tangent_gate, loss_weight=loss_weight)


def slope_of(gate_pre, up_pre):
    a = gate_pre.astype(jnp.float32)
    sig = jax.nn.sigmoid(a)
    return sig * (1.0 + a * (1.0 - sig)) * up_pre.astype(jnp.float32)


def reference(tokens, gate_pre, up_pre, down_weight, tangent_gate, loss_weight):
    slope = slope_of(gate_pre, up_pre)
    tangent_gate_out = jnp.dot(tokens, tangent_gate, preferred_element_type=jnp.float32)
    tangent_hidden = (slope * tangent_gate_out).astype(jnp.bfloat16)
    tangent_out = jnp.dot(tangent_hidden, down_weight, preferred_element_type=jnp.float32)
    weighted = (loss_weight[:, None] * tangent_out).astype(jnp.bfloat16)
    back_hidden = jnp.dot(weighted, down_weight.T, preferred_element_type=jnp.float32)
    back_gate = (back_hidden * slope).astype(jnp.bfloat16)
    token_blocks = tokens.reshape(N_BATCH, TOK_DEV, D)
    gate_blocks = back_gate.reshape(N_BATCH, TOK_DEV, FF)

    def accumulate(total, pair):
        block_tokens, block_gate = pair
        term = jnp.dot(block_tokens.T, block_gate, preferred_element_type=jnp.float32)
        rounded = lax.optimization_barrier(term.astype(jnp.bfloat16))
        return total + rounded.astype(jnp.float32), None

    gnvp, unused = lax.scan(accumulate, jnp.zeros((D, FF), jnp.float32), (token_blocks, gate_blocks))
    return gnvp
```

```python
import jax
import jax.numpy as jnp
from jax import lax
from jax.experimental import pallas as pl
from jax.experimental.pallas import tpu as pltpu
from jax.sharding import PartitionSpec as P

MESH = pl.DeviceIdType.MESH
TOK = 256
D = 4096
F = 448
FM = 384
COL = 128
ROWS = 896
ZCH = 4
CH = ROWS // ZCH


def slope_of(gate_pre, up_pre):
    a = gate_pre.astype(jnp.float32)
    sig = jax.nn.sigmoid(a)
    return sig * (1.0 + a * (1.0 - sig)) * up_pre.astype(jnp.float32)


def dot(a, b):
    return jnp.dot(a, b, preferred_element_type=jnp.float32)


def kernel(
    tok_in, gate_in, up_in, w_hbm, tan_in, lw_in, out_ref,
    tok, tokt, tan, relay_a, w, slope, hidden,
    part, merge, cross, quad, quad_in, pair_out, pair_in,
    wt, sib_out, sib_in, own, y_in, z_out, relay_d, z_in, acc, edges,
    send_sem, recv_sem, local_sem,
):
    b = lax.axis_index("batch")
    t = lax.axis_index("tensor")
    zh, y, c = b // 8, (b // 2) % 4, b % 2
    x, zl = t // 8, t % 8
    jq, jr = zl // 4, zl % 4
    z = zh * 8 + zl
    up = 1 - 2 * c

    def at(zh_=zh, y_=y, c_=c, x_=x, zl_=zl):
        return {"batch": zh_ * 8 + y_ * 2 + c_, "tensor": x_ * 8 + zl_}

    def at_z(z_):
        z_ = (z_ + 16) % 16
        return at(zh_=z_ // 8, zl_=z_ % 8)

    xs = [at(x_=(x + k) % 4) for k in range(4)]
    ys = [at(y_=(y + k) % 4) for k in range(4)]
    qs = [at(zl_=jq * 4 + (jr + k) % 4) for k in range(4)]
    pair = at(zl_=(zl + 4) % 8)
    sib = at(c_=1 - c)
    ahead = at_z(z + 4 * up)

    count = [0]
    sent = []

    def copy(src, dst, dev):
        i = count[0]
        count[0] += 1
        return pltpu.make_async_remote_copy(
            src_ref=src, dst_ref=dst, send_sem=send_sem.at[i], recv_sem=recv_sem.at[i],
            device_id=dev, device_id_type=MESH,
        )

    def send(src, dst, dev):
        cp = copy(src, dst, dev)
        cp.start()
        sent.append(cp)
        return count[0] - 1

    def arrived(dst, i):
        pltpu.make_async_remote_copy(
            src_ref=dst, dst_ref=dst, send_sem=send_sem.at[i], recv_sem=recv_sem.at[i],
            device_id=sib, device_id_type=MESH,
        ).wait_recv()

    w_copy = pltpu.make_async_copy(w_hbm, w, local_sem)
    w_copy.start()

    tcol = pl.multiple_of(t * COL, COL)
    tok[:, pl.ds(tcol, COL)] = tok_in[...]
    for i in range(3):
        tan[b, i * TOK : (i + 1) * TOK, :] = tan_in[:, i * COL : (i + 1) * COL]
    tan[b, 3 * TOK :, :] = jnp.concatenate([tan_in[0:128, FM:F], tan_in[128:256, FM:F]], axis=1)

    barrier = pltpu.get_barrier_semaphore()
    partners = xs[1:] + ys[1:] + qs[1:] + [sib, at_z(z + 4), at_z(z - 4)]
    for dev in partners:
        pl.semaphore_signal(barrier, inc=1, device_id=dev, device_id_type=MESH)
    pl.semaphore_wait(barrier, len(partners))

    class Gather:
        def __init__(self, buf):
            self.buf = buf
            self.x_ids = {}

        def piece(self, zp, xp=None, lo=0, n=TOK):
            col = pl.multiple_of(((x if xp is None else xp) * 8 + zp) * COL, COL)
            return self.buf.at[pl.ds(lo, n), pl.ds(col, COL)]

        def pz(self, h, k):
            return ((jq + h) % 2) * 4 + (jr + 4 - k) % 4

        def along_x(self, h, k):
            ref = self.piece(self.pz(h, k))
            self.x_ids[h, k] = [send(ref, ref, xs[1]), send(ref, ref, xs[3])]

        def start(self):
            ref = self.piece(zl)
            self.pair_id = send(ref, ref, pair)
            self.quad_ids = [[None] + [send(ref, ref, qs[k]) for k in (1, 2, 3)], None]
            self.along_x(0, 0)

        def take_pair(self):
            ref = self.piece(self.pz(1, 0))
            arrived(ref, self.pair_id)
            self.quad_ids[1] = [None] + [send(ref, ref, qs[k]) for k in (1, 2, 3)]
            self.along_x(1, 0)

        def take_quad(self, h, k):
            arrived(self.piece(self.pz(h, k)), self.quad_ids[h][k])
            self.along_x(h, k)

        def forward_x(self, h, k):
            zp = self.pz(h, k)
            left, right = (x + 3) % 4, (x + 1) % 4
            arrived(self.piece(zp, left), self.x_ids[h, k][0])
            lo = self.piece(zp, left, 0, TOK // 2)
            ids = [send(lo, lo, xs[1])]
            arrived(self.piece(zp, right), self.x_ids[h, k][1])
            hi = self.piece(zp, right, TOK // 2, TOK // 2)
            ids.append(send(hi, hi, xs[3]))
            self.x_ids[h, k] += ids

        def finish(self, h, k):
            zp = self.pz(h, k)
            far = (x + 2) % 4
            arrived(self.piece(zp, far, 0, TOK // 2), self.x_ids[h, k][2])
            arrived(self.piece(zp, far, TOK // 2, TOK // 2), self.x_ids[h, k][3])

    order = [(0, 0), (0, 1), (0, 2), (0, 3), (1, 0), (1, 1), (1, 2), (1, 3)]

    def chunk(ref, i, n=1):
        return ref.at[pl.ds(i * CH, n * CH), :]

    other = (1 - zh) * 8 + y * 2 + c
    z_src = (z - 4 * up + 16) % 16
    b_src = (z_src // 8) * 8 + y * 2 + c
    own_block = tan.at[b]
    leg1 = [send(chunk(own_block, i), chunk(relay_a, i), ahead) for i in range(ZCH)]
    g = Gather(tok)
    g.start()
    y_own = [None] + [send(own_block, own_block, ys[k]) for k in (1, 2, 3)]
    sib_ids = {}
    sib_ids[0, 0] = send(own_block, own_block, sib)

    slope[...] = slope_of(gate_in[...], up_in[...])

    g.take_pair()
    leg2 = []

    def pass_on(i):
        arrived(chunk(relay_a, i), leg1[i])
        leg2.append(send(chunk(relay_a, i), chunk(tan.at[b_src], i), ahead))

    pass_on(0)
    for k in (1, 2, 3):
        g.take_quad(0, k)
    pass_on(1)
    g.forward_x(0, 0)
    g.forward_x(1, 0)
    pass_on(2)
    for k in (1, 2, 3):
        g.take_quad(1, k)
        g.forward_x(0, k)
    pass_on(3)
    for k in (1, 2, 3):
        g.forward_x(1, k)

    def tan_slot(hz, k):
        return ((zh + hz) % 2) * 8 + ((y + 4 - k) % 4) * 2 + c

    for k in (1, 2, 3):
        ref = tan.at[tan_slot(0, k)]
        arrived(ref, y_own[k])
        sib_ids[0, k] = send(ref, ref, sib)
    y_other = []
    for half in range(2):
        for i in range(2):
            arrived(chunk(tan.at[other], 2 * half + i), leg2[2 * half + i])
        ref = chunk(tan.at[other], 2 * half, 2)
        y_other.append([None] + [send(ref, ref, ys[k]) for k in (1, 2, 3)])
    sib_ids[1, 0] = send(tan.at[other], tan.at[other], sib)
    for k in (1, 2, 3):
        block = tan.at[tan_slot(1, k)]
        arrived(chunk(block, 0, 2), y_other[0][k])
        arrived(chunk(block, 2, 2), y_other[1][k])
        sib_ids[1, k] = send(block, block, sib)
    for h, k in order:
        g.finish(h, k)
    for hz in range(2):
        for k in range(4):
            arrived(tan.at[((zh + hz) % 2) * 8 + ((y + 4 - k) % 4) * 2 + 1 - c], sib_ids[hz, k])

    acc[...] = jnp.zeros_like(acc)

    @pl.loop(0, 16)
    def _(i):
        cols = tok[:, pl.ds(pl.multiple_of(i * TOK, TOK), TOK)]
        main = jnp.concatenate(
            [tan[i, j * TOK : (j + 1) * TOK, :] for j in range(3)], axis=1
        )
        edge = tan[i, 3 * TOK :, :]
        acc[:, 0:FM] += dot(cols, main)
        acc[:, FM : FM + COL] += dot(cols[:, 0:128], edge)
        acc[:, FM + COL :] += dot(cols[:, 128:256], edge)

    hidden[:, 0:FM] = (slope[:, 0:FM] * acc[:, 0:FM]).astype(jnp.bfloat16)
    hidden[:, FM:F] = (
        slope[:, FM:F] * (acc[:, FM : FM + 64] + acc[:, FM + COL + 64 : FM + 2 * COL])
    ).astype(jnp.bfloat16)

    w_copy.wait()

    def zq(h, k):
        return ((jq + h) % 2) * 4 + (jr + k) % 4

    def p_ref(kx, h, k, lo=0, n=TOK):
        col = pl.multiple_of((((x + kx) % 4) * 8 + zq(h, k)) * COL, COL)
        return part.at[pl.ds(lo, n), pl.ds(col, COL)]

    rs = [(1, 1), (1, 2), (1, 3), (1, 0), (0, 1), (0, 2), (0, 3), (0, 0)]
    half = TOK // 2
    m_ids, c_ids, q_ids = {}, {}, {}
    for h in (1, 0):
        for kx in (2, 1, 3, 0):
            col = pl.multiple_of(((x + kx) % 4) * 1024 + ((jq + h) % 2) * 512, 512)
            part[:, pl.ds(col, 512)] = dot(hidden[...], w[:, pl.ds(col, 512)]).astype(jnp.bfloat16)
            if kx == 2:
                for k in (1, 2, 3, 0):
                    n = rs.index((h, k))
                    m_ids[h, k] = [
                        send(p_ref(2, h, k, 0, half), merge.at[0, n], xs[1]),
                        send(p_ref(2, h, k, half, half), merge.at[1, n], xs[3]),
                    ]

    def merge_x(h, k):
        n = rs.index((h, k))
        c_ids[h, k] = []
        for side, kx in ((0, 1), (1, 3)):
            arrived(merge.at[side, n], m_ids[h, k][side])
            ref = p_ref(kx, h, k, side * half, half)
            ref[...] = (
                ref[...].astype(jnp.float32) + merge[side, n].astype(jnp.float32)
            ).astype(jnp.bfloat16)
            c_ids[h, k].append(send(p_ref(kx, h, k), cross.at[side, n], xs[kx]))

    def reduce_x(h, k):
        n = rs.index((h, k))
        arrived(cross.at[0, n], c_ids[h, k][0])
        arrived(cross.at[1, n], c_ids[h, k][1])
        total = (
            p_ref(0, h, k)[...].astype(jnp.float32)
            + cross[0, n].astype(jnp.float32)
            + cross[1, n].astype(jnp.float32)
        )
        if k == 0:
            return total
        quad[n] = total.astype(jnp.bfloat16)
        q_ids[h, k] = send(quad.at[n], quad_in.at[n], qs[k])

    def reduce_quad(h, total):
        for k in (1, 2, 3):
            n = rs.index((h, k))
            arrived(quad_in.at[n], q_ids[h, k])
            total = total + quad_in[n].astype(jnp.float32)
        return total

    for h, k in rs[:6]:
        merge_x(h, k)
    for h, k in rs[:3]:
        reduce_x(h, k)
    for h, k in rs[6:]:
        merge_x(h, k)
    tot1 = reduce_x(1, 0)
    for h, k in rs[4:5]:
        reduce_x(h, k)
    pair_out[...] = reduce_quad(1, tot1).astype(jnp.bfloat16)
    pair_id = send(pair_out, pair_in, pair)
    for h, k in rs[5:7]:
        reduce_x(h, k)
    tot0 = reduce_x(0, 0)
    tot0 = reduce_quad(0, tot0)
    arrived(pair_in, pair_id)
    weight = jnp.transpose(jnp.broadcast_to(lw_in[...], (COL, TOK)))
    wt[:, pl.ds(tcol, COL)] = (
        weight * (tot0 + pair_in[...].astype(jnp.float32))
    ).astype(jnp.bfloat16)

    g = Gather(wt)
    g.start()

    @pl.loop(0, 16)
    def _(i):
        at_i = pl.ds(pl.multiple_of(i * TOK, TOK), TOK)
        tokt[at_i, :] = jnp.transpose(tok[:, at_i])

    g.take_pair()
    for k in (1, 2, 3):
        g.take_quad(0, k)
    g.forward_x(0, 0)
    g.forward_x(1, 0)
    for k in (1, 2, 3):
        g.take_quad(1, k)
        g.forward_x(0, k)
    for k in (1, 2, 3):
        g.forward_x(1, k)
    for h, k in order:
        g.finish(h, k)

    acc[:, 0:F] = jnp.zeros((TOK, F), jnp.float32)

    @pl.loop(0, 8)
    def _(i):
        at_i = pl.ds(pl.multiple_of(i * 512, 512), 512)
        acc[:, 0:F] += lax.dot_general(
            wt[:, at_i], w[:, at_i], (((1,), (1,)), ((), ())), preferred_element_type=jnp.float32
        )

    hidden[...] = (acc[:, 0:F] * slope[...]).astype(jnp.bfloat16)

    back = hidden[...]
    main = back[:, 0:FM]
    edge = back[:, FM:F]
    zero = jnp.zeros_like(edge)
    edges[:, 0:64] = edge
    edges[:, 64:128] = zero
    edges[:, 128:192] = zero
    edges[:, 192:256] = edge
    edge_lo, edge_hi = edges[:, 0:128], edges[:, 128:256]

    def product(blk, emit):
        row = pl.multiple_of(blk * TOK, TOK)
        top = dot(tokt[pl.ds(row, TOK), :], main)
        for j in range(3):
            emit(j * TOK, TOK, top[:, j * COL : (j + 1) * COL])
        low = dot(tokt[pl.ds(row, 128), :], edge_lo) + dot(tokt[pl.ds(row + 128, 128), :], edge_hi)
        emit(3 * TOK, 128, low)

    blocks = [(hz, ky) for hz in (1, 0) for ky in (2, 1, 3, 0)]
    s_ids, y_ids = {}, {}
    for n, (hz, ky) in enumerate(blocks):
        blk = ((zh + hz) % 2) * 8 + ((y + ky) % 4) * 2 + 1 - c

        def emit(lo, rows, val):
            sib_out[n, lo : lo + rows, :] = val.astype(jnp.bfloat16)

        product(blk, emit)
        s_ids[hz, ky] = send(sib_out.at[n], sib_in.at[n], sib)
    for n, (hz, ky) in enumerate(blocks):
        blk = ((zh + hz) % 2) * 8 + ((y + ky) % 4) * 2 + c
        arrived(sib_in.at[n], s_ids[hz, ky])

        def emit(lo, rows, val):
            own[n, lo : lo + rows, :] = (
                val + sib_in[n, lo : lo + rows, :].astype(jnp.float32)
            ).astype(jnp.bfloat16)

        product(blk, emit)
        if ky:
            parts = ZCH if hz else 1
            y_ids[hz, ky] = [
                send(chunk(own.at[n], i, ZCH // parts), chunk(y_in.at[n], i, ZCH // parts), ys[ky])
                for i in range(parts)
            ]

    def rows_of(ref, n, lo, rows):
        return ref[n, lo : lo + rows, :].astype(jnp.float32)

    leg1, leg2 = [], []
    for i in range(ZCH):
        lo = i * CH
        total = rows_of(own, 3, lo, CH)
        for n in range(3):
            arrived(chunk(y_in.at[n], i), y_ids[blocks[n]][i])
            total = total + rows_of(y_in, n, lo, CH)
        z_out[lo : lo + CH, :] = total.astype(jnp.bfloat16)
        leg1.append(send(chunk(z_out, i), chunk(relay_d, i), ahead))
    for i in range(ZCH):
        arrived(chunk(relay_d, i), leg1[i])
        leg2.append(send(chunk(relay_d, i), chunk(z_in, i), ahead))
    for n in range(4, 7):
        arrived(y_in.at[n], y_ids[blocks[n]][0])
    for i in range(ZCH):
        arrived(chunk(z_in, i), leg2[i])

    def final(lo, rows):
        total = rows_of(own, 7, lo, rows) + z_in[lo : lo + rows, :].astype(jnp.float32)
        for n in range(4, 7):
            total = total + rows_of(y_in, n, lo, rows)
        return total

    for j in range(3):
        out_ref[:, j * COL : (j + 1) * COL] = final(j * TOK, TOK)
    low = final(3 * TOK, 128)
    out_ref[0:128, FM:F] = low[:, 0:64]
    out_ref[128:256, FM:F] = low[:, 64:128]

    for cp in sent:
        cp.wait_send()


N_SEM = 192


def body(tokens, gate_pre, up_pre, down_weight, tangent_gate, loss_weight):
    vmem = pl.BlockSpec(memory_space=pltpu.VMEM)
    bf = jnp.bfloat16
    return pl.pallas_call(
        kernel,
        out_shape=jax.ShapeDtypeStruct((TOK, F), jnp.float32),
        in_specs=[vmem, vmem, vmem, pl.BlockSpec(memory_space=pl.ANY), vmem, vmem],
        out_specs=vmem,
        scratch_shapes=[
            pltpu.VMEM((TOK, D), bf),
            pltpu.VMEM((D, TOK), bf),
            pltpu.VMEM((16, ROWS, COL), bf),
            pltpu.VMEM((ROWS, COL), bf),
            pltpu.VMEM((F, D), bf),
            pltpu.VMEM((TOK, F), jnp.float32),
            pltpu.VMEM((TOK, F), bf),
            pltpu.VMEM((TOK, D), bf),
            pltpu.VMEM((2, 8, TOK // 2, COL), bf),
            pltpu.VMEM((2, 8, TOK, COL), bf),
            pltpu.VMEM((8, TOK, COL), bf),
            pltpu.VMEM((8, TOK, COL), bf),
            pltpu.VMEM((TOK, COL), bf),
            pltpu.VMEM((TOK, COL), bf),
            pltpu.VMEM((TOK, D), bf),
            pltpu.VMEM((8, ROWS, COL), bf),
            pltpu.VMEM((8, ROWS, COL), bf),
            pltpu.VMEM((8, ROWS, COL), bf),
            pltpu.VMEM((8, ROWS, COL), bf),
            pltpu.VMEM((ROWS, COL), bf),
            pltpu.VMEM((ROWS, COL), bf),
            pltpu.VMEM((ROWS, COL), bf),
            pltpu.VMEM((TOK, FM + 2 * COL), jnp.float32),
            pltpu.VMEM((TOK, 2 * COL), bf),
            pltpu.SemaphoreType.DMA((N_SEM,)),
            pltpu.SemaphoreType.DMA((N_SEM,)),
            pltpu.SemaphoreType.DMA,
        ],
        compiler_params=pltpu.CompilerParams(
            collective_id=0, has_side_effects=True, vmem_limit_bytes=56 * 2**20
        ),
    )(tokens, gate_pre, up_pre, down_weight, tangent_gate, loss_weight.reshape(1, TOK))


def solution(mesh):
    placed = (
        P("batch", "tensor"),
        P("batch", "tensor"),
        P("batch", "tensor"),
        P("tensor", None),
        P("batch", "tensor"),
        P("batch"),
    )
    return jax.shard_map(
        body, mesh=mesh, in_specs=placed, out_specs=P("batch", "tensor"), check_vma=False
    )
```

```python
import jax
import jax.numpy as jnp
from jax import lax
from jax.experimental import pallas as pl
from jax.experimental.pallas import tpu as pltpu
from jax.sharding import PartitionSpec as P

MESH = pl.DeviceIdType.MESH
TOK = 256
D = 4096
F = 448
COL = 128
ZCH = 4
CH = F // ZCH
NT = (((1,), (1,)), ((), ()))


def slope_of(gate_pre, up_pre):
    a = gate_pre.astype(jnp.float32)
    sig = jax.nn.sigmoid(a)
    return sig * (1.0 + a * (1.0 - sig)) * up_pre.astype(jnp.float32)


def dot(a, b):
    return jnp.dot(a, b, preferred_element_type=jnp.float32)


def kernel(
    tok_in, gate_in, up_in, w_hbm, tan_in, lw_in, out_ref,
    tok, tan, relay_a, w, slope, hidden,
    part, merge, cross, quad, quad_in, pair_out, pair_in,
    wt, tok_sib, back, back_in, own, y_in, z_out, relay_d, z_in, acc,
    send_sem, recv_sem, local_sem,
):
    b = lax.axis_index("batch")
    t = lax.axis_index("tensor")
    zh, y, c = b // 8, (b // 2) % 4, b % 2
    x, zl = t // 8, t % 8
    jq, jr = zl // 4, zl % 4
    z = zh * 8 + zl
    up = 1 - 2 * c

    def at(zh_=zh, y_=y, c_=c, x_=x, zl_=zl):
        return {"batch": zh_ * 8 + y_ * 2 + c_, "tensor": x_ * 8 + zl_}

    def at_z(z_):
        z_ = (z_ + 16) % 16
        return at(zh_=z_ // 8, zl_=z_ % 8)

    xs = [at(x_=(x + k) % 4) for k in range(4)]
    ys = [at(y_=(y + k) % 4) for k in range(4)]
    qs = [at(zl_=jq * 4 + (jr + k) % 4) for k in range(4)]
    pair = at(zl_=(zl + 4) % 8)
    sib = at(c_=1 - c)
    ahead = at_z(z + 4 * up)

    count = [0]
    sent = []

    def copy(src, dst, dev):
        i = count[0]
        count[0] += 1
        return pltpu.make_async_remote_copy(
            src_ref=src, dst_ref=dst, send_sem=send_sem.at[i], recv_sem=recv_sem.at[i],
            device_id=dev, device_id_type=MESH,
        )

    def send(src, dst, dev):
        cp = copy(src, dst, dev)
        cp.start()
        sent.append(cp)
        return count[0] - 1

    def arrived(dst, i):
        pltpu.make_async_remote_copy(
            src_ref=dst, dst_ref=dst, send_sem=send_sem.at[i], recv_sem=recv_sem.at[i],
            device_id=sib, device_id_type=MESH,
        ).wait_recv()

    w_copy = pltpu.make_async_copy(w_hbm, w, local_sem)
    w_copy.start()

    tcol = pl.multiple_of(t * COL, COL)
    tok[:, pl.ds(tcol, COL)] = tok_in[...]
    tan[b] = tan_in[...]

    barrier = pltpu.get_barrier_semaphore()
    partners = xs[1:] + ys[1:] + qs[1:] + [sib, at_z(z + 4), at_z(z - 4)]
    for dev in partners:
        pl.semaphore_signal(barrier, inc=1, device_id=dev, device_id_type=MESH)
    pl.semaphore_wait(barrier, len(partners))

    class Gather:
        def __init__(self, buf):
            self.buf = buf
            self.x_ids = {}

        def piece(self, zp, xp=None, lo=0, n=TOK):
            col = pl.multiple_of(((x if xp is None else xp) * 8 + zp) * COL, COL)
            return self.buf.at[pl.ds(lo, n), pl.ds(col, COL)]

        def pz(self, h, k):
            return ((jq + h) % 2) * 4 + (jr + 4 - k) % 4

        def along_x(self, h, k):
            ref = self.piece(self.pz(h, k))
            self.x_ids[h, k] = [send(ref, ref, xs[1]), send(ref, ref, xs[3])]

        def start(self):
            ref = self.piece(zl)
            self.pair_id = send(ref, ref, pair)
            self.quad_ids = [[None] + [send(ref, ref, qs[k]) for k in (1, 2, 3)], None]
            self.along_x(0, 0)

        def take_pair(self):
            ref = self.piece(self.pz(1, 0))
            arrived(ref, self.pair_id)
            self.quad_ids[1] = [None] + [send(ref, ref, qs[k]) for k in (1, 2, 3)]
            self.along_x(1, 0)

        def take_quad(self, h, k):
            arrived(self.piece(self.pz(h, k)), self.quad_ids[h][k])
            self.along_x(h, k)

        def forward_x(self, h, k):
            zp = self.pz(h, k)
            left, right = (x + 3) % 4, (x + 1) % 4
            arrived(self.piece(zp, left), self.x_ids[h, k][0])
            lo = self.piece(zp, left, 0, TOK // 2)
            ids = [send(lo, lo, xs[1])]
            arrived(self.piece(zp, right), self.x_ids[h, k][1])
            hi = self.piece(zp, right, TOK // 2, TOK // 2)
            ids.append(send(hi, hi, xs[3]))
            self.x_ids[h, k] += ids

        def finish(self, h, k):
            zp = self.pz(h, k)
            far = (x + 2) % 4
            arrived(self.piece(zp, far, 0, TOK // 2), self.x_ids[h, k][2])
            arrived(self.piece(zp, far, TOK // 2, TOK // 2), self.x_ids[h, k][3])

    order = [(0, 0), (0, 1), (0, 2), (0, 3), (1, 0), (1, 1), (1, 2), (1, 3)]

    def chunk(ref, i, n=1):
        return ref.at[pl.ds(i * CH, n * CH), :]

    other = (1 - zh) * 8 + y * 2 + c
    z_src = (z - 4 * up + 16) % 16
    b_src = (z_src // 8) * 8 + y * 2 + c
    own_block = tan.at[b]
    leg1 = [send(chunk(own_block, i), chunk(relay_a, i), ahead) for i in range(ZCH)]
    g = Gather(tok)
    g.start()
    sib_own = [send(own_block, own_block, sib), None, None, None]

    slope[...] = slope_of(gate_in[...], up_in[...])

    def tan_slot(hz, k, c_=c):
        return ((zh + hz) % 2) * 8 + ((y + 4 - k) % 4) * 2 + c_

    leg2, y_other, sib_other = [], [], [[None] * ZCH for _ in range(4)]

    def pass_on(i):
        arrived(chunk(relay_a, i), leg1[i])
        leg2.append(send(chunk(relay_a, i), chunk(tan.at[b_src], i), ahead))

    def spread(i):
        ref = chunk(tan.at[other], i)
        arrived(ref, leg2[i])
        y_other.append([None] + [send(ref, ref, ys[k]) for k in (1, 2, 3)])
        sib_other[0][i] = send(ref, ref, sib)

    def share_own(k):
        ref = tan.at[tan_slot(0, k)]
        arrived(ref, y_own[k])
        sib_own[k] = send(ref, ref, sib)

    def share_other(k, i):
        ref = chunk(tan.at[tan_slot(1, k)], i)
        arrived(ref, y_other[i][k])
        sib_other[k][i] = send(ref, ref, sib)

    g.take_pair()
    pass_on(0)
    y_own = [None] + [send(own_block, own_block, ys[k]) for k in (1, 2, 3)]
    for k in (1, 2, 3):
        g.take_quad(0, k)
        pass_on(k)
    for k in (1, 3, 2):
        share_own(k)
    for k in (1, 2, 3):
        g.take_quad(1, k)
    spread(0)
    g.forward_x(0, 0)
    g.forward_x(1, 0)
    spread(1)
    for k in (1, 2, 3):
        g.forward_x(0, k)
    spread(2)
    for k in (1, 2, 3):
        g.forward_x(1, k)
    spread(3)
    for i in range(ZCH):
        for k in (1, 3, 2):
            share_other(k, i)
    for h, k in order:
        g.finish(h, k)
    for k in range(4):
        arrived(tan.at[tan_slot(0, k, 1 - c)], sib_own[k])

    def tangent_part(first):
        lhs = jnp.concatenate([tan[first + j] for j in range(4)], axis=1)
        rhs = tok[:, pl.ds(pl.multiple_of(first * TOK, 4 * TOK), 4 * TOK)]
        return lax.dot_general(lhs, rhs, NT, preferred_element_type=jnp.float32)

    acc[...] = tangent_part(zh * 8)
    acc[...] += tangent_part(zh * 8 + 4)
    for k in range(4):
        for i in range(ZCH):
            arrived(chunk(tan.at[tan_slot(1, k, 1 - c)], i), sib_other[k][i])
    acc[...] += tangent_part((1 - zh) * 8)
    tgo = acc[...] + tangent_part((1 - zh) * 8 + 4)
    hidden[...] = jnp.transpose((slope[...] * tgo).astype(jnp.bfloat16))

    tok_id = send(tok, tok_sib, sib)
    w_copy.wait()

    def zq(h, k):
        return ((jq + h) % 2) * 4 + (jr + k) % 4

    def p_ref(kx, h, k, lo=0, n=TOK):
        col = pl.multiple_of((((x + kx) % 4) * 8 + zq(h, k)) * COL, COL)
        return part.at[pl.ds(lo, n), pl.ds(col, COL)]

    rs = [(1, 1), (1, 2), (1, 3), (1, 0), (0, 1), (0, 2), (0, 3), (0, 0)]
    half = TOK // 2
    m_ids, c_ids, q_ids = {}, {}, {}
    for h in (1, 0):
        for kx in (2, 1, 3, 0):
            col = pl.multiple_of(((x + kx) % 4) * 1024 + ((jq + h) % 2) * 512, 512)
            part[:, pl.ds(col, 512)] = dot(hidden[...], w[:, pl.ds(col, 512)]).astype(jnp.bfloat16)
            if kx == 2:
                for k in (1, 2, 3, 0):
                    n = rs.index((h, k))
                    m_ids[h, k] = [
                        send(p_ref(2, h, k, 0, half), merge.at[0, n], xs[1]),
                        send(p_ref(2, h, k, half, half), merge.at[1, n], xs[3]),
                    ]

    def merge_x(h, k):
        n = rs.index((h, k))
        c_ids[h, k] = []
        for side, kx in ((0, 1), (1, 3)):
            arrived(merge.at[side, n], m_ids[h, k][side])
            ref = p_ref(kx, h, k, side * half, half)
            ref[...] = (
                ref[...].astype(jnp.float32) + merge[side, n].astype(jnp.float32)
            ).astype(jnp.bfloat16)
            c_ids[h, k].append(send(p_ref(kx, h, k), cross.at[side, n], xs[kx]))

    def reduce_x(h, k):
        n = rs.index((h, k))
        arrived(cross.at[0, n], c_ids[h, k][0])
        arrived(cross.at[1, n], c_ids[h, k][1])
        total = (
            p_ref(0, h, k)[...].astype(jnp.float32)
            + cross[0, n].astype(jnp.float32)
            + cross[1, n].astype(jnp.float32)
        )
        if k == 0:
            return total
        quad[n] = total.astype(jnp.bfloat16)
        q_ids[h, k] = send(quad.at[n], quad_in.at[n], qs[k])

    def reduce_quad(h, total):
        for k in (1, 2, 3):
            n = rs.index((h, k))
            arrived(quad_in.at[n], q_ids[h, k])
            total = total + quad_in[n].astype(jnp.float32)
        return total

    for h, k in rs[:4]:
        merge_x(h, k)
    for h, k in rs[:3]:
        reduce_x(h, k)
    tot1 = reduce_x(1, 0)
    for h, k in rs[4:]:
        merge_x(h, k)
    pair_out[...] = reduce_quad(1, tot1).astype(jnp.bfloat16)
    pair_id = send(pair_out, pair_in, pair)
    for h, k in rs[4:7]:
        reduce_x(h, k)
    tot0 = reduce_x(0, 0)
    tot0 = reduce_quad(0, tot0)
    arrived(pair_in, pair_id)
    weight = jnp.transpose(jnp.broadcast_to(lw_in[...], (COL, TOK)))
    wt[:, pl.ds(tcol, COL)] = (
        weight * (tot0 + pair_in[...].astype(jnp.float32))
    ).astype(jnp.bfloat16)

    g = Gather(wt)
    g.start()

    def back_part(xp):
        cols = pl.ds(pl.multiple_of(xp * 1024, 1024), 1024)
        return lax.dot_general(w[:, cols], wt[:, cols], NT, preferred_element_type=jnp.float32)

    g.take_pair()
    for k in (1, 2, 3):
        g.take_quad(0, k)
    for k in (1, 2, 3):
        g.take_quad(1, k)
    g.forward_x(0, 0)
    g.forward_x(1, 0)
    acc[...] = back_part(x)
    for k in (1, 2, 3):
        g.forward_x(0, k)
    for k in (1, 2, 3):
        g.forward_x(1, k)
    acc[...] += back_part((x + 1) % 4)
    acc[...] += back_part((x + 3) % 4)
    for h, k in order:
        g.finish(h, k)

    back_hidden = acc[...] + back_part((x + 2) % 4)
    back[...] = (back_hidden * slope[...]).astype(jnp.bfloat16)

    back_id = send(back, back_in, sib)
    arrived(tok_sib, tok_id)
    arrived(back_in, back_id)
    y_ids = {}

    def to_y(hz):
        for i in (0, 2):
            rows = slice(i * CH, (i + 2) * CH)
            lhs = jnp.concatenate([back[rows, :], back_in[rows, :]], axis=1)
            for ky in (2, 1, 3, 0):
                blk = ((zh + hz) % 2) * 8 + ((y + ky) % 4) * 2 + c
                cols = pl.ds(pl.multiple_of(blk * TOK, TOK), TOK)
                term = dot(lhs, jnp.concatenate([tok[:, cols], tok_sib[:, cols]], axis=0))
                for j in (0, 1):
                    own[hz, i + j, ky] = term[j * CH : (j + 1) * CH].astype(jnp.bfloat16)
                    if ky:
                        ref = own.at[hz, i + j, ky]
                        y_ids[hz, ky, i + j] = send(ref, y_in.at[hz, i + j, ky], ys[ky])

    def y_sum(hz, i):
        total = own[hz, i, 0].astype(jnp.float32)
        for ky in (1, 3, 2):
            arrived(y_in.at[hz, i, ky], y_ids[hz, ky, i])
            total = total + y_in[hz, i, ky].astype(jnp.float32)
        return total

    chunks = range(ZCH)
    to_y(1)
    leg1, leg2 = [], []
    for i in chunks:
        z_out[i * CH : (i + 1) * CH, :] = y_sum(1, i).astype(jnp.bfloat16)
        leg1.append(send(chunk(z_out, i), chunk(relay_d, i), ahead))
    to_y(0)
    for i in chunks:
        arrived(chunk(relay_d, i), leg1[i])
        leg2.append(send(chunk(relay_d, i), chunk(z_in, i), ahead))
    for i in chunks:
        out_ref[i * CH : (i + 1) * CH, :] = y_sum(0, i)
    for i in chunks:
        arrived(chunk(z_in, i), leg2[i])
        out_ref[i * CH : (i + 1) * CH, :] += z_in[i * CH : (i + 1) * CH, :].astype(jnp.float32)

    for cp in sent:
        cp.wait_send()


N_SEM = 208


def body(tokens, gate_pre, up_pre, down_weight, tangent_gate, loss_weight):
    vmem = pl.BlockSpec(memory_space=pltpu.VMEM)
    bf = jnp.bfloat16
    return pl.pallas_call(
        kernel,
        out_shape=jax.ShapeDtypeStruct((F, TOK), jnp.float32),
        in_specs=[vmem, vmem, vmem, pl.BlockSpec(memory_space=pl.ANY), vmem, vmem],
        out_specs=vmem,
        scratch_shapes=[
            pltpu.VMEM((TOK, D), bf),
            pltpu.VMEM((16, F, TOK), bf),
            pltpu.VMEM((F, TOK), bf),
            pltpu.VMEM((F, D), bf),
            pltpu.VMEM((F, TOK), jnp.float32),
            pltpu.VMEM((TOK, F), bf),
            pltpu.VMEM((TOK, D), bf),
            pltpu.VMEM((2, 8, TOK // 2, COL), bf),
            pltpu.VMEM((2, 8, TOK, COL), bf),
            pltpu.VMEM((8, TOK, COL), bf),
            pltpu.VMEM((8, TOK, COL), bf),
            pltpu.VMEM((TOK, COL), bf),
            pltpu.VMEM((TOK, COL), bf),
            pltpu.VMEM((TOK, D), bf),
            pltpu.VMEM((TOK, D), bf),
            pltpu.VMEM((F, TOK), bf),
            pltpu.VMEM((F, TOK), bf),
            pltpu.VMEM((2, ZCH, 4, CH, TOK), bf),
            pltpu.VMEM((2, ZCH, 4, CH, TOK), bf),
            pltpu.VMEM((F, TOK), bf),
            pltpu.VMEM((F, TOK), bf),
            pltpu.VMEM((F, TOK), bf),
            pltpu.VMEM((F, TOK), jnp.float32),
            pltpu.SemaphoreType.DMA((N_SEM,)),
            pltpu.SemaphoreType.DMA((N_SEM,)),
            pltpu.SemaphoreType.DMA,
        ],
        compiler_params=pltpu.CompilerParams(
            collective_id=0, has_side_effects=True, vmem_limit_bytes=56 * 2**20
        ),
    )(
        tokens, gate_pre.T, up_pre.T, down_weight, tangent_gate.T, loss_weight.reshape(1, TOK)
    ).T


def solution(mesh):
    placed = (
        P("batch", "tensor"),
        P("batch", "tensor"),
        P("batch", "tensor"),
        P("tensor", None),
        P("batch", "tensor"),
        P("batch"),
    )
    return jax.shard_map(
        body, mesh=mesh, in_specs=placed, out_specs=P("batch", "tensor"), check_vma=False
    )
```

```python
import jax
import jax.numpy as jnp
from jax import lax
from jax.experimental import pallas as pl
from jax.experimental.pallas import tpu as pltpu
from jax.sharding import PartitionSpec as P

MESH = pl.DeviceIdType.MESH
TOK = 256
D = 4096
F = 448
COL = 128
ZCH = 4
CH = F // ZCH
NT = (((1,), (1,)), ((), ()))


def slope_of(gate_pre, up_pre):
    a = gate_pre.astype(jnp.float32)
    sig = jax.nn.sigmoid(a)
    return sig * (1.0 + a * (1.0 - sig)) * up_pre.astype(jnp.float32)


def dot(a, b):
    return jnp.dot(a, b, preferred_element_type=jnp.float32)


def kernel(
    tok_in, gate_in, up_in, w_hbm, tan_in, lw_in, out_ref, z_in,
    tok, tan, relay_a, w, slope, hidden,
    part, merge, cross, quad, quad_in, pair_out, pair_in,
    wt, tok_sib, back, back_in, own, y_in, z_out, relay_d, acc,
    send_sem, recv_sem, local_sem,
):
    b = lax.axis_index("batch")
    t = lax.axis_index("tensor")
    zh, y, c = b // 8, (b // 2) % 4, b % 2
    x, zl = t // 8, t % 8
    jq, jr = zl // 4, zl % 4
    z = zh * 8 + zl
    up = 1 - 2 * c

    def at(zh_=zh, y_=y, c_=c, x_=x, zl_=zl):
        return {"batch": zh_ * 8 + y_ * 2 + c_, "tensor": x_ * 8 + zl_}

    def at_z(z_):
        z_ = (z_ + 16) % 16
        return at(zh_=z_ // 8, zl_=z_ % 8)

    xs = [at(x_=(x + k) % 4) for k in range(4)]
    ys = [at(y_=(y + k) % 4) for k in range(4)]
    qs = [at(zl_=jq * 4 + (jr + k) % 4) for k in range(4)]
    pair = at(zl_=(zl + 4) % 8)
    sib = at(c_=1 - c)
    ahead = at_z(z + 4 * up)

    count = [0]
    sent = []

    def copy(src, dst, dev):
        i = count[0]
        count[0] += 1
        return pltpu.make_async_remote_copy(
            src_ref=src, dst_ref=dst, send_sem=send_sem.at[i], recv_sem=recv_sem.at[i],
            device_id=dev, device_id_type=MESH,
        )

    def send(src, dst, dev):
        cp = copy(src, dst, dev)
        cp.start()
        sent.append(cp)
        return count[0] - 1

    def arrived(dst, i):
        pltpu.make_async_remote_copy(
            src_ref=dst, dst_ref=dst, send_sem=send_sem.at[i], recv_sem=recv_sem.at[i],
            device_id=sib, device_id_type=MESH,
        ).wait_recv()

    w_copy = pltpu.make_async_copy(w_hbm, w, local_sem)
    w_copy.start()

    tcol = pl.multiple_of(t * COL, COL)
    tok[:, pl.ds(tcol, COL)] = tok_in[...]
    tan[b] = tan_in[...]

    barrier = pltpu.get_barrier_semaphore()
    partners = xs[1:] + ys[1:] + qs[1:] + [sib, at_z(z + 4), at_z(z - 4)]
    for dev in partners:
        pl.semaphore_signal(barrier, inc=1, device_id=dev, device_id_type=MESH)
    pl.semaphore_wait(barrier, len(partners))

    class Gather:
        def __init__(self, buf):
            self.buf = buf
            self.x_ids = {}

        def piece(self, zp, xp=None, lo=0, n=TOK):
            col = pl.multiple_of(((x if xp is None else xp) * 8 + zp) * COL, COL)
            return self.buf.at[pl.ds(lo, n), pl.ds(col, COL)]

        def pz(self, h, k):
            return ((jq + h) % 2) * 4 + (jr + 4 - k) % 4

        def along_x(self, h, k):
            ref = self.piece(self.pz(h, k))
            self.x_ids[h, k] = [send(ref, ref, xs[1]), send(ref, ref, xs[3])]

        def start(self):
            ref = self.piece(zl)
            self.pair_id = send(ref, ref, pair)
            self.quad_ids = [[None] + [send(ref, ref, qs[k]) for k in (1, 2, 3)], None]
            self.along_x(0, 0)

        def take_pair(self):
            ref = self.piece(self.pz(1, 0))
            arrived(ref, self.pair_id)
            self.quad_ids[1] = [None] + [send(ref, ref, qs[k]) for k in (1, 2, 3)]
            self.along_x(1, 0)

        def take_quad(self, h, k):
            arrived(self.piece(self.pz(h, k)), self.quad_ids[h][k])
            self.along_x(h, k)

        def forward_x(self, h, k):
            zp = self.pz(h, k)
            left, right = (x + 3) % 4, (x + 1) % 4
            arrived(self.piece(zp, left), self.x_ids[h, k][0])
            lo = self.piece(zp, left, 0, TOK // 2)
            ids = [send(lo, lo, xs[1])]
            arrived(self.piece(zp, right), self.x_ids[h, k][1])
            hi = self.piece(zp, right, TOK // 2, TOK // 2)
            ids.append(send(hi, hi, xs[3]))
            self.x_ids[h, k] += ids

        def finish(self, h, k):
            zp = self.pz(h, k)
            far = (x + 2) % 4
            arrived(self.piece(zp, far, 0, TOK // 2), self.x_ids[h, k][2])
            arrived(self.piece(zp, far, TOK // 2, TOK // 2), self.x_ids[h, k][3])

    order = [(0, 0), (0, 1), (0, 2), (0, 3), (1, 0), (1, 1), (1, 2), (1, 3)]

    def chunk(ref, i, n=1):
        return ref.at[pl.ds(i * CH, n * CH), :]

    other = (1 - zh) * 8 + y * 2 + c
    z_src = (z - 4 * up + 16) % 16
    b_src = (z_src // 8) * 8 + y * 2 + c
    own_block = tan.at[b]
    leg1 = [send(chunk(own_block, i), chunk(relay_a, i), ahead) for i in range(ZCH)]
    g = Gather(tok)
    g.start()
    sib_own = [send(own_block, own_block, sib), None, None, None]

    slope[...] = slope_of(gate_in[...], up_in[...])

    def tan_slot(hz, k, c_=c):
        return ((zh + hz) % 2) * 8 + ((y + 4 - k) % 4) * 2 + c_

    leg2, y_other, sib_other = [], [], [[None] * ZCH for _ in range(4)]

    def pass_on(i):
        arrived(chunk(relay_a, i), leg1[i])
        leg2.append(send(chunk(relay_a, i), chunk(tan.at[b_src], i), ahead))

    def spread(i):
        ref = chunk(tan.at[other], i)
        arrived(ref, leg2[i])
        y_other.append([None] + [send(ref, ref, ys[k]) for k in (1, 2, 3)])
        sib_other[0][i] = send(ref, ref, sib)

    def share_own(k):
        ref = tan.at[tan_slot(0, k)]
        arrived(ref, y_own[k])
        sib_own[k] = send(ref, ref, sib)

    def share_other(k, i):
        ref = chunk(tan.at[tan_slot(1, k)], i)
        arrived(ref, y_other[i][k])
        sib_other[k][i] = send(ref, ref, sib)

    g.take_pair()
    pass_on(0)
    y_own = [None] + [send(own_block, own_block, ys[k]) for k in (1, 2, 3)]
    for k in (1, 2, 3):
        g.take_quad(0, k)
        pass_on(k)
    for k in (1, 3, 2):
        share_own(k)
    for k in (1, 2, 3):
        g.take_quad(1, k)
    spread(0)
    g.forward_x(0, 0)
    g.forward_x(1, 0)
    spread(1)
    for k in (1, 2, 3):
        g.forward_x(0, k)
    spread(2)
    for k in (1, 2, 3):
        g.forward_x(1, k)
    spread(3)
    for i in range(ZCH):
        for k in (1, 3, 2):
            share_other(k, i)
    for h, k in order:
        g.finish(h, k)
    for k in range(4):
        arrived(tan.at[tan_slot(0, k, 1 - c)], sib_own[k])

    def tangent_part(first):
        lhs = jnp.concatenate([tan[first + j] for j in range(4)], axis=1)
        rhs = tok[:, pl.ds(pl.multiple_of(first * TOK, 4 * TOK), 4 * TOK)]
        return lax.dot_general(lhs, rhs, NT, preferred_element_type=jnp.float32)

    acc[...] = tangent_part(zh * 8)
    acc[...] += tangent_part(zh * 8 + 4)
    for k in range(4):
        for i in range(ZCH):
            arrived(chunk(tan.at[tan_slot(1, k, 1 - c)], i), sib_other[k][i])
    acc[...] += tangent_part((1 - zh) * 8)
    tgo = acc[...] + tangent_part((1 - zh) * 8 + 4)
    hidden[...] = jnp.transpose((slope[...] * tgo).astype(jnp.bfloat16))

    tok_ids = {}

    def tok_block(buf, n, c_):
        return buf.at[:, pl.ds(pl.multiple_of((2 * n + c_) * TOK, TOK), TOK)]

    def share_tok(first, n):
        for j in range(first, first + n):
            tok_ids[j] = send(tok_block(tok, j, 1 - c), tok_block(tok_sib, j, 1 - c), sib)

    w_copy.wait()

    def zq(h, k):
        return ((jq + h) % 2) * 4 + (jr + k) % 4

    def p_ref(kx, h, k, lo=0, n=TOK):
        col = pl.multiple_of((((x + kx) % 4) * 8 + zq(h, k)) * COL, COL)
        return part.at[pl.ds(lo, n), pl.ds(col, COL)]

    rs = [(1, 1), (1, 2), (1, 3), (1, 0), (0, 1), (0, 2), (0, 3), (0, 0)]
    half = TOK // 2
    m_ids, c_ids, q_ids = {}, {}, {}
    for h in (1, 0):
        for kx in (2, 1, 3, 0):
            col = pl.multiple_of(((x + kx) % 4) * 1024 + ((jq + h) % 2) * 512, 512)
            part[:, pl.ds(col, 512)] = dot(hidden[...], w[:, pl.ds(col, 512)]).astype(jnp.bfloat16)
            if kx == 2:
                for k in (1, 2, 3, 0):
                    n = rs.index((h, k))
                    m_ids[h, k] = [
                        send(p_ref(2, h, k, 0, half), merge.at[0, n], xs[1]),
                        send(p_ref(2, h, k, half, half), merge.at[1, n], xs[3]),
                    ]

    def merge_x(h, k):
        n = rs.index((h, k))
        c_ids[h, k] = []
        for side, kx in ((0, 1), (1, 3)):
            arrived(merge.at[side, n], m_ids[h, k][side])
            ref = p_ref(kx, h, k, side * half, half)
            ref[...] = (
                ref[...].astype(jnp.float32) + merge[side, n].astype(jnp.float32)
            ).astype(jnp.bfloat16)
            c_ids[h, k].append(send(p_ref(kx, h, k), cross.at[side, n], xs[kx]))

    def reduce_x(h, k):
        n = rs.index((h, k))
        arrived(cross.at[0, n], c_ids[h, k][0])
        arrived(cross.at[1, n], c_ids[h, k][1])
        total = (
            p_ref(0, h, k)[...].astype(jnp.float32)
            + cross[0, n].astype(jnp.float32)
            + cross[1, n].astype(jnp.float32)
        )
        if k == 0:
            return total
        quad[n] = total.astype(jnp.bfloat16)
        q_ids[h, k] = send(quad.at[n], quad_in.at[n], qs[k])

    def reduce_quad(h, total):
        for k in (1, 2, 3):
            n = rs.index((h, k))
            arrived(quad_in.at[n], q_ids[h, k])
            total = total + quad_in[n].astype(jnp.float32)
        return total

    for h, k in rs[:4]:
        merge_x(h, k)
    for h, k in rs[:3]:
        reduce_x(h, k)
    tot1 = reduce_x(1, 0)
    for h, k in rs[4:]:
        merge_x(h, k)
    pair_out[...] = reduce_quad(1, tot1).astype(jnp.bfloat16)
    pair_id = send(pair_out, pair_in, pair)
    for h, k in rs[4:7]:
        reduce_x(h, k)
    tot0 = reduce_x(0, 0)
    tot0 = reduce_quad(0, tot0)
    arrived(pair_in, pair_id)
    weight = jnp.transpose(jnp.broadcast_to(lw_in[...], (COL, TOK)))
    wt[:, pl.ds(tcol, COL)] = (
        weight * (tot0 + pair_in[...].astype(jnp.float32))
    ).astype(jnp.bfloat16)

    g = Gather(wt)
    g.start()

    def back_part(xp):
        cols = pl.ds(pl.multiple_of(xp * 1024, 1024), 1024)
        return lax.dot_general(w[:, cols], wt[:, cols], NT, preferred_element_type=jnp.float32)

    g.take_pair()
    for k in (1, 2, 3):
        g.take_quad(0, k)
    for k in (1, 2, 3):
        g.take_quad(1, k)
    g.forward_x(0, 0)
    g.forward_x(1, 0)
    acc[...] = back_part(x)
    for k in (1, 2, 3):
        g.forward_x(0, k)
    for k in (1, 2, 3):
        g.forward_x(1, k)
    share_tok(0, 8)
    acc[...] += back_part((x + 1) % 4)
    acc[...] += back_part((x + 3) % 4)
    for h, k in order:
        g.finish(h, k)

    back_hidden = acc[...] + back_part((x + 2) % 4)
    back[...] = (back_hidden * slope[...]).astype(jnp.bfloat16)

    back_id = send(back, back_in, sib)
    for n in range(8):
        arrived(tok_block(tok_sib, n, c), tok_ids[n])
    arrived(back_in, back_id)
    y_ids = {}

    def to_y(hz):
        for i in range(4):
            rows = slice(i * CH, (i + 1) * CH)
            lhs = jnp.concatenate([back[rows, :], back_in[rows, :]], axis=1)
            for ky in (2, 1, 3, 0):
                blk = ((zh + hz) % 2) * 8 + ((y + ky) % 4) * 2 + c
                cols = pl.ds(pl.multiple_of(blk * TOK, TOK), TOK)
                term = dot(lhs, jnp.concatenate([tok[:, cols], tok_sib[:, cols]], axis=0))
                for j in (0,):
                    own[hz, i + j, ky] = term[j * CH : (j + 1) * CH].astype(jnp.bfloat16)
                    if ky:
                        ref = own.at[hz, i + j, ky]
                        y_ids[hz, ky, i + j] = send(ref, y_in.at[hz, i + j, ky], ys[ky])

    def y_sum(hz, i):
        total = own[hz, i, 0].astype(jnp.float32)
        for ky in (1, 3, 2):
            arrived(y_in.at[hz, i, ky], y_ids[hz, ky, i])
            total = total + y_in[hz, i, ky].astype(jnp.float32)
        return total

    chunks = range(ZCH)
    to_y(1)
    leg1, leg2 = [], []
    for i in chunks:
        z_out[i * CH : (i + 1) * CH, :] = y_sum(1, i).astype(jnp.bfloat16)
        leg1.append(send(chunk(z_out, i), chunk(relay_d, i), ahead))
    to_y(0)
    for i in chunks:
        arrived(chunk(relay_d, i), leg1[i])
        leg2.append(send(chunk(relay_d, i), chunk(z_in, i), ahead))
    for i in chunks:
        out_ref[i * CH : (i + 1) * CH, :] = y_sum(0, i)
    for i in chunks:
        arrived(chunk(z_in, i), leg2[i])

    for cp in sent:
        cp.wait_send()


N_SEM = 208


def body(tokens, gate_pre, up_pre, down_weight, tangent_gate, loss_weight):
    vmem = pl.BlockSpec(memory_space=pltpu.VMEM)
    bf = jnp.bfloat16
    near, far = pl.pallas_call(
        kernel,
        out_shape=[
            jax.ShapeDtypeStruct((F, TOK), jnp.float32),
            jax.ShapeDtypeStruct((F, TOK), bf),
        ],
        in_specs=[vmem, vmem, vmem, pl.BlockSpec(memory_space=pl.ANY), vmem, vmem],
        out_specs=[vmem, vmem],
        scratch_shapes=[
            pltpu.VMEM((TOK, D), bf),
            pltpu.VMEM((16, F, TOK), bf),
            pltpu.VMEM((F, TOK), bf),
            pltpu.VMEM((F, D), bf),
            pltpu.VMEM((F, TOK), jnp.float32),
            pltpu.VMEM((TOK, F), bf),
            pltpu.VMEM((TOK, D), bf),
            pltpu.VMEM((2, 8, TOK // 2, COL), bf),
            pltpu.VMEM((2, 8, TOK, COL), bf),
            pltpu.VMEM((8, TOK, COL), bf),
            pltpu.VMEM((8, TOK, COL), bf),
            pltpu.VMEM((TOK, COL), bf),
            pltpu.VMEM((TOK, COL), bf),
            pltpu.VMEM((TOK, D), bf),
            pltpu.VMEM((TOK, D), bf),
            pltpu.VMEM((F, TOK), bf),
            pltpu.VMEM((F, TOK), bf),
            pltpu.VMEM((2, ZCH, 4, CH, TOK), bf),
            pltpu.VMEM((2, ZCH, 4, CH, TOK), bf),
            pltpu.VMEM((F, TOK), bf),
            pltpu.VMEM((F, TOK), bf),
            pltpu.VMEM((F, TOK), jnp.float32),
            pltpu.SemaphoreType.DMA((N_SEM,)),
            pltpu.SemaphoreType.DMA((N_SEM,)),
            pltpu.SemaphoreType.DMA,
        ],
        compiler_params=pltpu.CompilerParams(
            collective_id=0, has_side_effects=True, vmem_limit_bytes=56 * 2**20
        ),
    )(
        tokens, gate_pre.T, up_pre.T, down_weight, tangent_gate.T, loss_weight.reshape(1, TOK)
    )
    return (near + far.astype(jnp.float32)).T


def solution(mesh):
    placed = (
        P("batch", "tensor"),
        P("batch", "tensor"),
        P("batch", "tensor"),
        P("tensor", None),
        P("batch", "tensor"),
        P("batch"),
    )
    return jax.shard_map(
        body, mesh=mesh, in_specs=placed, out_specs=P("batch", "tensor"), check_vma=False
    )
```
